768 devices in a mesh: fsdp: 24 (over z, core), tensor: 32 (over y, x).
Axes of the slice: x: 4, y: 8, z: 12, core: 2. Of those that a mesh axis runs over, the one named last changes fastest.
Arguments:
- momentum: float32 [12288, 16384], P('fsdp', 'tensor'), may hold values from -60 to 60
- gradient: bfloat16 [12288, 16384], P('fsdp', 'tensor'), may hold values from -6 to 6
- basis: float32 [16384, 128], P('tensor'), may hold values from -6 to 6
- weight: bfloat16 [12288, 16384], P('fsdp', 'tensor'), may hold values from -3 to 3
Outputs:
- momentum_next: float32 [12288, 16384], P('fsdp', 'tensor')
- basis_next: float32 [16384, 128], P('tensor')
- weight_next: bfloat16 [12288, 16384], P('fsdp', 'tensor')
The draws below stay inside these ranges and needn't reach their ends.
All inputs are finite; a program needn't handle non-finite values.
Results may differ from the reference program's by a relative error of at most 0.001.
Values sent between devices are 32-bit elements; how exact they have to be, the bound alone decides.
No kernel may reach another device: no remote copies, remote signals or barrier semaphores. Data moves between devices by JAX's collectives and lax.ppermute only.
A program may use at most 32 MiB of HBM per device.

```python
import jax
import jax.numpy as jnp
from jax import lax

COLS = 16384
RANK = 128
ROWS = 12288


def draw_momentum(key, part):
    key = jax.random.fold_in(key, 11)
    keys = jax.random.split(key, 3)
    row_pos = jnp.arange(ROWS, dtype=jnp.float32) / ROWS
    col_pos = jnp.arange(COLS, dtype=jnp.float32) / COLS
    row_scale = 10.0 ** (0.75 * row_pos + 0.25 * jax.random.uniform(keys[0], (ROWS,), jnp.float32))
    col_scale = 10.0 ** (0.75 * col_pos + 0.25 * jax.random.uniform(keys[1], (COLS,), jnp.float32))
    base = jax.random.normal(keys[2], (ROWS, COLS), jnp.float32)
    base = jnp.clip(base, -6.0, 6.0)
    return (0.1 * base * row_scale[:, None] * col_scale[None, :]).astype(jnp.float32)


def block_levels(own_key, extent, pieces, smallest, high):
    factor_of = 1.0
    for axis_at, shards_of in pieces:
        steps = jax.random.uniform(jax.random.fold_in(jax.random.fold_in(own_key, 6), axis_at), (shards_of,), jnp.float32, smallest / len(pieces), high / len(pieces))
        factor_of = factor_of * jnp.repeat(jnp.exp(steps), extent[axis_at] // shards_of).reshape((-1,) + (1,) * (len(extent) - 1 - axis_at))
    return factor_of


def bell_draw(stream_key, dims, deviation, most, pieces=(), kind=jnp.bfloat16):
    loudness = block_levels(stream_key, dims, pieces, -0.22, 0.18) if pieces else 1.0
    array = jax.random.normal(stream_key, dims, jnp.float32) * deviation * loudness
    return jnp.minimum(jnp.maximum(array, -most), most).astype(kind)


def setup_inputs(seed: int = 0) -> dict:
    splits = jax.random.split(jax.random.key(seed), 5)
    return {
        "momentum": draw_momentum(jax.random.fold_in(splits[4], 71), 0),
        "gradient": bell_draw(splits[1], (ROWS, COLS), 1.0, 6.0, ((0, 24), (1, 32))),
        "basis": bell_draw(splits[2], (COLS, RANK), 1.0, 6.0, ((0, 32),), jnp.float32),
        "weight": bell_draw(splits[3], (ROWS, COLS), 0.2, 3.0, ((0, 24), (1, 32))),
    }


def reference(momentum, gradient, basis, weight):
    high = lax.Precision.HIGHEST
    blend = momentum + gradient.astype(jnp.float32)
    projected = jnp.dot(blend, basis, precision=high)
    gram = jnp.dot(projected.T, projected, precision=high)
    factor = jnp.linalg.cholesky(gram)
    ortho = jax.scipy.linalg.solve_triangular(factor, projected.T, lower=True).T
    right = jnp.dot(blend.T, ortho, precision=high)
    colsq = lax.optimization_barrier(jnp.sum(right * right, axis=0))
    basis_next = right / jnp.sqrt(colsq / COLS + 1e-06)
    momentum_next = blend - 0.05 * jnp.dot(ortho, right.T, precision=high)
    update = jnp.sqrt(jnp.float32(ROWS) / RANK) * jnp.dot(ortho, basis_next.T, precision=high)
    weight_next = (weight.astype(jnp.float32) - 0.05 * update).astype(jnp.bfloat16)
    return (momentum_next, basis_next, weight_next)
```

```python
import jax
import jax.numpy as jnp
from jax import lax
from jax.sharding import Mesh, PartitionSpec as P

ROWS_AXES = ("z", "core")
COLS_AXES = ("y", "x")
HIGH = lax.Precision.HIGHEST
SUBLANES = 8


def scatter_sum(parts, axes):
    return jnp.sum(lax.all_to_all(parts, axes, 0, 0), axis=0)


def gather(part, axes):
    size = lax.axis_size(axes)
    return lax.all_to_all(jnp.broadcast_to(part[None], (size, *part.shape)), axes, 0, 0)


def sum_over_rows(array):
    height, width = array.shape
    half = height // 2
    core = lax.axis_index("core")
    swap = [(0, 1), (1, 0)]
    kept = lax.dynamic_slice_in_dim(array, core * half, half)
    sent = lax.dynamic_slice_in_dim(array, (1 - core) * half, half)
    kept = kept + lax.ppermute(sent, "core", swap)
    ring = lax.axis_size("z")
    share = -(-half // (ring * SUBLANES)) * SUBLANES
    kept = jnp.pad(kept, ((0, ring * share - half), (0, 0)))
    share_sum = scatter_sum(kept.reshape(ring, share, width), "z")
    mine = gather(share_sum, "z").reshape(ring * share, width)[:half]
    other = lax.ppermute(mine, "core", swap)
    first = core == 0
    return jnp.concatenate([jnp.where(first, mine, other), jnp.where(first, other, mine)])


def shards(momentum, gradient, basis, weight):
    rows, cols = momentum.shape
    rank = basis.shape[1]
    n_cols = lax.axis_size(COLS_AXES)
    total_rows = rows * lax.axis_size(ROWS_AXES)
    total_cols = cols * n_cols

    blend = momentum + gradient.astype(jnp.float32)
    partial_rows = jnp.dot(blend, basis, precision=HIGH)
    my_rows = scatter_sum(partial_rows.reshape(n_cols, rows // n_cols, rank), COLS_AXES)
    projected = gather(my_rows, COLS_AXES).reshape(rows, rank)

    raw_right = jnp.dot(blend.T, projected, precision=HIGH)
    gram = jnp.dot(projected.T, projected, precision=HIGH)
    sums = sum_over_rows(jnp.concatenate([raw_right, gram]))
    raw_right, gram = sums[:cols], sums[cols:]

    factor = jnp.linalg.cholesky(gram)
    inverse = jax.scipy.linalg.solve_triangular(factor, jnp.eye(rank, dtype=jnp.float32), lower=True)
    right = jnp.dot(raw_right, inverse.T, precision=HIGH)
    colsq = jnp.sum(gather(jnp.sum(right * right, axis=0, keepdims=True), COLS_AXES), axis=(0, 1))
    ortho = jnp.dot(projected, inverse.T, precision=HIGH)

    basis_next = right / jnp.sqrt(colsq / total_cols + 1e-06)
    momentum_next = blend - 0.05 * jnp.dot(ortho, right.T, precision=HIGH)
    update = jnp.sqrt(jnp.float32(total_rows) / rank) * jnp.dot(ortho, basis_next.T, precision=HIGH)
    weight_next = (weight.astype(jnp.float32) - 0.05 * update).astype(jnp.bfloat16)
    return (momentum_next, basis_next, weight_next)


def split(mesh, x_size):
    n_rows, n_cols = mesh.devices.shape
    return Mesh(mesh.devices.reshape(n_rows // 2, 2, n_cols // x_size, x_size), ROWS_AXES + COLS_AXES)


def solution(mesh, x_size=4):
    block = P(ROWS_AXES, COLS_AXES)
    factor_block = P(COLS_AXES, None)
    return jax.shard_map(
        shards,
        mesh=split(mesh, x_size),
        in_specs=(block, block, factor_block, block),
        out_specs=(block, factor_block, block),
        check_vma=False,
    )
```

```python
import jax
import jax.numpy as jnp
from jax import lax
from jax.experimental import pallas as pl
from jax.sharding import Mesh, PartitionSpec as P

ROWS_AXES = ("z", "core")
COLS_AXES = ("y", "x")
HIGH = lax.Precision.HIGHEST
SUBLANES = 8
LANES = 128


def scatter_sum(parts, axes):
    return jnp.sum(lax.all_to_all(parts, axes, 0, 0), axis=0)


def gather(part, axes):
    size = lax.axis_size(axes)
    return lax.all_to_all(jnp.broadcast_to(part[None], (size, *part.shape)), axes, 0, 0)


def sum_over_rows(right, gram):
    height, width = right.shape
    half = height // 2
    core = lax.axis_index("core")
    swap = [(0, 1), (1, 0)]
    kept = lax.dynamic_slice_in_dim(right, core * half, half)
    sent = lax.dynamic_slice_in_dim(right, (1 - core) * half, half)
    sums = jnp.concatenate([kept, gram])
    sums = sums + lax.ppermute(jnp.concatenate([sent, gram]), "core", swap)
    ring = lax.axis_size("z")
    used = sums.shape[0]
    share = -(-used // (ring * SUBLANES)) * SUBLANES
    sums = jnp.pad(sums, ((0, ring * share - used), (0, 0)))
    sums = gather(scatter_sum(sums.reshape(ring, share, width), "z"), "z").reshape(ring * share, width)
    return sums[:used], lax.ppermute(sums[:half], "core", swap)


def spread(value):
    return jnp.broadcast_to(value, (SUBLANES, value.shape[-1] if value.shape[-1] > 1 else LANES))


def inverse_factor(strips):
    strips = list(strips)
    lane = lax.broadcasted_iota(jnp.int32, (SUBLANES, LANES), 1)
    row = lax.broadcasted_iota(jnp.int32, (SUBLANES, LANES), 0)
    block = range(SUBLANES)
    done = []
    for k in range(LANES // SUBLANES):
        first = k * SUBLANES
        rows = [spread(strips[k][c : c + 1, :]) for c in block]
        left = [[spread(rows[c][:, first + m : first + m + 1]) for m in range(c + 1)] for c in block]
        lower = [[None] * SUBLANES for _ in block]
        inverse = [None] * SUBLANES
        for c in block:
            inverse[c] = 1.0 / left[c][c]
            for i in range(c + 1, SUBLANES):
                lower[i][c] = left[i][c] * inverse[c]
            for i in range(c + 1, SUBLANES):
                for m in range(c + 1, i + 1):
                    left[i][m] = left[i][m] - lower[i][c] * left[m][c]
        inside = (lane >= first) & (lane < first + SUBLANES)
        forward = []
        for c in block:
            value = jnp.where(inside, jnp.where(lane == first + c, 1.0, 0.0), rows[c])
            for m in range(c):
                value = value - lower[c][m] * forward[m]
            forward.append(value)
        solved = [None] * SUBLANES
        for c in reversed(block):
            value = forward[c] * inverse[c]
            for i in range(SUBLANES - 1, c, -1):
                value = value - lower[i][c] * solved[i]
            solved[c] = value
        for b in range(k + 1, LANES // SUBLANES):
            value = jnp.where(inside, 0.0, strips[b])
            for c in block:
                value = value - spread(strips[b][:, first + c : first + c + 1]) * solved[c]
            strips[b] = value
        unit, pivots = forward[0], left[0][0]
        for c in range(1, SUBLANES):
            unit = jnp.where(row == c, forward[c], unit)
            pivots = jnp.where(row == c, left[c][c], pivots)
        done.append(jnp.where(lane <= row + first, unit, 0.0) * lax.rsqrt(pivots))
    return done


def inverse_factor_kernel(sums_ref, inverse_ref):
    top = sums_ref.shape[0] - LANES
    strips = [sums_ref[top + r : top + r + SUBLANES, :] for r in range(0, LANES, SUBLANES)]
    for r, strip in enumerate(inverse_factor(strips)):
        inverse_ref[r * SUBLANES : (r + 1) * SUBLANES, :] = strip


def invert_gram(sums):
    return pl.pallas_call(
        inverse_factor_kernel,
        out_shape=jax.ShapeDtypeStruct((LANES, LANES), jnp.float32),
        cost_estimate=pl.CostEstimate(flops=6_000_000_000, bytes_accessed=200_000, transcendentals=20_000),
    )(sums)


def shards(momentum, gradient, basis, weight):
    rows, cols = momentum.shape
    rank = basis.shape[1]
    n_cols = lax.axis_size(COLS_AXES)
    total_rows = rows * lax.axis_size(ROWS_AXES)
    total_cols = cols * n_cols

    blend = momentum + gradient.astype(jnp.float32)
    partial_rows = jnp.dot(blend, basis, precision=HIGH)
    my_rows = scatter_sum(partial_rows.reshape(n_cols, rows // n_cols, rank), COLS_AXES)
    projected = gather(my_rows, COLS_AXES).reshape(rows, rank)

    raw_right = jnp.dot(blend.T, projected, precision=HIGH)
    gram = jnp.dot(projected.T, projected, precision=HIGH)
    sums, other = sum_over_rows(raw_right, gram)
    inverse = invert_gram(sums)
    mine = sums[: cols // 2]
    first = lax.axis_index("core") == 0
    raw_right = jnp.concatenate([jnp.where(first, mine, other), jnp.where(first, other, mine)])
    right = jnp.dot(raw_right, inverse.T, precision=HIGH)
    colsq = jnp.sum(gather(jnp.sum(right * right, axis=0, keepdims=True), COLS_AXES), axis=(0, 1))
    ortho = jnp.dot(projected, inverse.T, precision=HIGH)

    basis_next = right / jnp.sqrt(colsq / total_cols + 1e-06)
    momentum_next = blend - 0.05 * jnp.dot(ortho, right.T, precision=HIGH)
    update = jnp.sqrt(jnp.float32(total_rows) / rank) * jnp.dot(ortho, basis_next.T, precision=HIGH)
    weight_next = (weight.astype(jnp.float32) - 0.05 * update).astype(jnp.bfloat16)
    return (momentum_next, basis_next, weight_next)


def split(mesh, x_size):
    n_rows, n_cols = mesh.devices.shape
    return Mesh(mesh.devices.reshape(n_rows // 2, 2, n_cols // x_size, x_size), ROWS_AXES + COLS_AXES)


def solution(mesh, x_size=4):
    block = P(ROWS_AXES, COLS_AXES)
    factor_block = P(COLS_AXES, None)
    return jax.shard_map(
        shards,
        mesh=split(mesh, x_size),
        in_specs=(block, block, factor_block, block),
        out_specs=(block, factor_block, block),
        check_vma=False,
    )
```

```python
import jax
import jax.numpy as jnp
from jax import lax
from jax.experimental import pallas as pl
from jax.experimental.pallas import tpu as pltpu
from jax.sharding import Mesh, PartitionSpec as P

ROWS_AXES = ("z", "core")
COLS_AXES = ("y", "x")
HIGH = lax.Precision.HIGHEST
SUBLANES = 8
LANES = 128
SWAP = [(0, 1), (1, 0)]


WHOLE = pl.BlockSpec(memory_space=pltpu.VMEM)


def near_shape(shape):
    return pltpu.VMEM(shape, jnp.float32)


def near(array):
    return pltpu.with_memory_space_constraint(array, pltpu.VMEM)


def sum_and_copy_kernel(parts_ref, copies_ref):
    total = parts_ref[0]
    for d in range(1, parts_ref.shape[0]):
        total = total + parts_ref[d]
    for d in range(copies_ref.shape[0]):
        copies_ref[d] = total


def all_sum(parts, axes):
    parts = lax.all_to_all(parts, axes, 0, 0)
    copies = pl.pallas_call(
        sum_and_copy_kernel,
        in_specs=[WHOLE],
        out_specs=WHOLE,
        out_shape=near_shape(parts.shape),
        cost_estimate=pl.CostEstimate(flops=parts.size, bytes_accessed=8 * parts.size, transcendentals=0),
    )(near(parts))
    return lax.all_to_all(copies, axes, 0, 0)


def gather(part, axes):
    size = lax.axis_size(axes)
    return lax.all_to_all(jnp.broadcast_to(part[None], (size, *part.shape)), axes, 0, 0)


def sum_over_rows(sent, kept, gram):
    half, width = kept.shape
    sums = jnp.concatenate([kept, gram]) + lax.ppermute(jnp.concatenate([sent, gram]), "core", SWAP)
    ring = lax.axis_size("z")
    used = sums.shape[0]
    share = -(-used // (ring * SUBLANES)) * SUBLANES
    sums = jnp.pad(sums, ((0, ring * share - used), (0, 0)))
    sums = all_sum(sums.reshape(ring, share, width), "z").reshape(ring * share, width)
    return sums[:used], lax.ppermute(sums[:half], "core", SWAP)


def spread(value):
    return jnp.broadcast_to(value, (SUBLANES, value.shape[-1] if value.shape[-1] > 1 else LANES))


def inverse_factor(strips):
    strips = list(strips)
    lane = lax.broadcasted_iota(jnp.int32, (SUBLANES, LANES), 1)
    row = lax.broadcasted_iota(jnp.int32, (SUBLANES, LANES), 0)
    block = range(SUBLANES)
    done = []
    for k in range(LANES // SUBLANES):
        first = k * SUBLANES
        rows = [spread(strips[k][c : c + 1, :]) for c in block]
        left = [[spread(rows[c][:, first + m : first + m + 1]) for m in range(c + 1)] for c in block]
        lower = [[None] * SUBLANES for _ in block]
        inverse = [None] * SUBLANES
        for c in block:
            inverse[c] = 1.0 / left[c][c]
            for i in range(c + 1, SUBLANES):
                lower[i][c] = left[i][c] * inverse[c]
            for i in range(c + 1, SUBLANES):
                for m in range(c + 1, i + 1):
                    left[i][m] = left[i][m] - lower[i][c] * left[m][c]
        inside = (lane >= first) & (lane < first + SUBLANES)
        forward = []
        for c in block:
            value = jnp.where(inside, jnp.where(lane == first + c, 1.0, 0.0), rows[c])
            for m in range(c):
                value = value - lower[c][m] * forward[m]
            forward.append(value)
        solved = [None] * SUBLANES
        for c in reversed(block):
            value = forward[c] * inverse[c]
            for i in range(SUBLANES - 1, c, -1):
                value = value - lower[i][c] * solved[i]
            solved[c] = value
        for b in range(k + 1, LANES // SUBLANES):
            value = jnp.where(inside, 0.0, strips[b])
            for c in block:
                value = value - spread(strips[b][:, first + c : first + c + 1]) * solved[c]
            strips[b] = value
        unit, pivots = forward[0], left[0][0]
        for c in range(1, SUBLANES):
            unit = jnp.where(row == c, forward[c], unit)
            pivots = jnp.where(row == c, left[c][c], pivots)
        done.append(jnp.where(lane <= row + first, unit, 0.0) * lax.rsqrt(pivots))
    return done


def inverse_factor_kernel(sums_ref, inverse_ref):
    top = sums_ref.shape[0] - LANES
    strips = [sums_ref[top + r : top + r + SUBLANES, :] for r in range(0, LANES, SUBLANES)]
    for r, strip in enumerate(inverse_factor(strips)):
        inverse_ref[r * SUBLANES : (r + 1) * SUBLANES, :] = strip


def invert_gram(sums):
    return pl.pallas_call(
        inverse_factor_kernel,
        in_specs=[WHOLE],
        out_specs=WHOLE,
        out_shape=near_shape((LANES, LANES)),
        cost_estimate=pl.CostEstimate(flops=6_000_000_000, bytes_accessed=200_000, transcendentals=20_000),
    )(near(sums))


def shards(momentum, gradient, basis, weight):
    rows, cols = momentum.shape
    rank = basis.shape[1]
    n_cols = lax.axis_size(COLS_AXES)
    total_rows = rows * lax.axis_size(ROWS_AXES)
    total_cols = cols * n_cols

    half = cols // 2
    blend = momentum + gradient.astype(jnp.float32)
    partial_rows = jnp.dot(blend, basis, precision=HIGH)
    first, partial_rows = lax.optimization_barrier((lax.axis_index("core") == 0, partial_rows))
    projected = all_sum(partial_rows.reshape(n_cols, rows // n_cols, rank), COLS_AXES).reshape(rows, rank)

    gram = jnp.dot(projected.T, projected, precision=HIGH)
    sent = jnp.dot(jnp.where(first, blend[:, half:], blend[:, :half]).T, projected, precision=HIGH)
    kept = jnp.dot(jnp.where(first, blend[:, :half], blend[:, half:]).T, projected, precision=HIGH)
    sums, other = sum_over_rows(sent, kept, gram)
    inverse = invert_gram(sums)
    mine = sums[:half]
    raw_right = jnp.concatenate([jnp.where(first, mine, other), jnp.where(first, other, mine)])
    right = jnp.dot(raw_right, inverse.T, precision=HIGH)
    colsq = jnp.sum(gather(jnp.sum(right * right, axis=0, keepdims=True), COLS_AXES), axis=(0, 1))
    late_inverse, right = lax.optimization_barrier((inverse, right))
    ortho = jnp.dot(projected, late_inverse.T, precision=HIGH)

    basis_next = right / jnp.sqrt(colsq / total_cols + 1e-06)
    momentum_next = blend - 0.05 * jnp.dot(ortho, right.T, precision=HIGH)
    update = jnp.sqrt(jnp.float32(total_rows) / rank) * jnp.dot(ortho, basis_next.T, precision=HIGH)
    weight_next = (weight.astype(jnp.float32) - 0.05 * update).astype(jnp.bfloat16)
    return (momentum_next, basis_next, weight_next)


def split(mesh, x_size):
    n_rows, n_cols = mesh.devices.shape
    return Mesh(mesh.devices.reshape(n_rows // 2, 2, n_cols // x_size, x_size), ROWS_AXES + COLS_AXES)


def solution(mesh, x_size=4):
    block = P(ROWS_AXES, COLS_AXES)
    factor_block = P(COLS_AXES, None)
    return jax.shard_map(
        shards,
        mesh=split(mesh, x_size),
        in_specs=(block, block, factor_block, block),
        out_specs=(block, factor_block, block),
        check_vma=False,
    )
```

```python
import functools

import jax
import jax.numpy as jnp
from jax import lax
from jax.experimental import pallas as pl
from jax.experimental.pallas import tpu as pltpu
from jax.sharding import Mesh, PartitionSpec as P

ROWS_AXES = ("z", "core")
COLS_AXES = ("y", "x")
HIGH = lax.Precision.HIGHEST
SUBLANES = 8
VMEM_LIMIT = 32 * 1024 * 1024
LANES = 128
SWAP = [(0, 1), (1, 0)]


WHOLE = pl.BlockSpec(memory_space=pltpu.VMEM)
FAR = pl.BlockSpec(memory_space=pltpu.HBM)
ROWS_BY_COLS = ((1,), (0,))
ROWS_BY_ROWS = ((1,), (1,))
COLS_BY_COLS = ((0,), (0,))


def near_shape(shape):
    return pltpu.VMEM(shape, jnp.float32)


def near(array):
    return pltpu.with_memory_space_constraint(array, pltpu.VMEM)


def far(array):
    return pltpu.with_memory_space_constraint(array, pltpu.HBM)


def estimate(flops, bytes_accessed):
    return pl.CostEstimate(flops=flops, bytes_accessed=bytes_accessed, transcendentals=0)


def product(left, right, dims, precision=None):
    return lax.dot_general(left, right, (dims, ((), ())), precision=precision, preferred_element_type=jnp.float32)


def high_low(array):
    high = array.astype(jnp.bfloat16)
    return high, (array - high.astype(jnp.float32)).astype(jnp.bfloat16)


def pair(array):
    return jnp.concatenate(high_low(array), axis=1)


def split_product(left, right_pair, dims):
    high, low = high_low(left)
    total = product(high, right_pair, dims) + product(low, right_pair, dims)
    width = total.shape[1] // 2
    return total[:, :width] + total[:, width:]


def project_kernel(momentum_ref, gradient_ref, basis_ref, blend_ref, partial_ref, momentum, gradient, basis, sems):
    copies = [
        pltpu.make_async_copy(basis_ref, basis, sems.at[0]),
        pltpu.make_async_copy(momentum_ref, momentum, sems.at[1]),
        pltpu.make_async_copy(gradient_ref, gradient, sems.at[2]),
    ]
    for copy in copies:
        copy.start()
    copies[0].wait()
    basis_pair = pair(basis[...])
    copies[1].wait()
    copies[2].wait()
    blend = momentum[...] + gradient[...].astype(jnp.float32)
    blend_ref[...] = blend
    partial_ref[...] = split_product(blend, basis_pair, ROWS_BY_COLS)


def project(momentum, gradient, basis):
    return pl.pallas_call(
        project_kernel,
        in_specs=[FAR] * 3,
        out_specs=[WHOLE] * 2,
        out_shape=[near_shape(momentum.shape), near_shape((momentum.shape[0], basis.shape[1]))],
        scratch_shapes=[
            pltpu.VMEM(momentum.shape, momentum.dtype),
            pltpu.VMEM(gradient.shape, gradient.dtype),
            pltpu.VMEM(basis.shape, basis.dtype),
            pltpu.SemaphoreType.DMA((3,)),
        ],
        compiler_params=pltpu.CompilerParams(vmem_limit_bytes=VMEM_LIMIT),
        cost_estimate=estimate(2 * momentum.size * basis.shape[1], 8 * momentum.size),
    )(far(momentum), far(gradient), far(basis))


def half_of(ref, core):
    half = ref.shape[1] // 2
    return ref[:, pl.ds(pl.multiple_of(core * half, half), half)]


def sent_kernel(blend_ref, projected_ref, sent_ref):
    projected = projected_ref[...]
    half = blend_ref.shape[1] // 2
    blend = half_of(blend_ref, 1 - lax.axis_index("core"))
    sent_ref[:half, :] = split_product(blend, pair(projected), COLS_BY_COLS)
    sent_ref[half:, :] = product(projected, projected, COLS_BY_COLS, HIGH)


def kept_kernel(blend_ref, projected_ref, kept_ref):
    blend = half_of(blend_ref, lax.axis_index("core"))
    kept_ref[...] = split_product(blend, pair(projected_ref[...]), COLS_BY_COLS)


def right_terms(kernel, height, blend, projected):
    return pl.pallas_call(
        kernel,
        in_specs=[WHOLE] * 2,
        out_specs=WHOLE,
        out_shape=near_shape((height, projected.shape[1])),
        compiler_params=pltpu.CompilerParams(vmem_limit_bytes=VMEM_LIMIT),
        cost_estimate=estimate(blend.size * projected.shape[1], 4 * blend.size),
    )(near(blend), near(projected))


def sum_and_copy_kernel(parts_ref, copies_ref):
    total = parts_ref[0]
    for d in range(1, parts_ref.shape[0]):
        total = total + parts_ref[d]
    for d in range(copies_ref.shape[0]):
        copies_ref[d] = total


def all_sum(parts, axes):
    parts = lax.all_to_all(parts, axes, 0, 0)
    copies = pl.pallas_call(
        sum_and_copy_kernel,
        in_specs=[WHOLE],
        out_specs=WHOLE,
        out_shape=near_shape(parts.shape),
        cost_estimate=pl.CostEstimate(flops=parts.size, bytes_accessed=8 * parts.size, transcendentals=0),
    )(near(parts))
    return lax.all_to_all(copies, axes, 0, 0)


def sum_over_rows(blend, projected):
    half, width = blend.shape[1] // 2, projected.shape[1]
    sent = right_terms(sent_kernel, half + width, blend, projected)
    arrived = lax.ppermute(sent, "core", SWAP)
    kept = right_terms(kept_kernel, half, blend, projected)
    sums = jnp.concatenate([kept, sent[half:]]) + arrived
    ring = lax.axis_size("z")
    used = sums.shape[0]
    share = -(-used // (ring * SUBLANES)) * SUBLANES
    sums = jnp.pad(sums, ((0, ring * share - used), (0, 0)))
    sums = all_sum(sums.reshape(ring, share, width), "z").reshape(ring * share, width)[:used]
    return sums, lax.ppermute(sums[:half], "core", SWAP)


def spread(value):
    return jnp.broadcast_to(value, (SUBLANES, value.shape[-1] if value.shape[-1] > 1 else LANES))


def tree_sum(terms):
    terms = list(terms)
    while len(terms) > 1:
        terms = [sum(terms[i : i + 2][1:], terms[i]) for i in range(0, len(terms), 2)]
    return terms[0]


def inverse_factor(strips):
    lane = lax.broadcasted_iota(jnp.int32, (SUBLANES, LANES), 1)
    row = lax.broadcasted_iota(jnp.int32, (SUBLANES, LANES), 0)
    block = range(SUBLANES)
    diagonals = [jnp.where(lane == row + k * SUBLANES, strip, 0.0) for k, strip in enumerate(strips)]
    across = lax.rsqrt(spread(jnp.sum(tree_sum(diagonals), axis=0, keepdims=True)))
    strips = [
        strip * lax.rsqrt(spread(jnp.sum(diagonal, axis=1, keepdims=True))) * across
        for strip, diagonal in zip(strips, diagonals)
    ]
    done = []
    for k in range(LANES // SUBLANES):
        first = k * SUBLANES
        inside = (lane >= first) & (lane < first + SUBLANES)
        rows = [spread(strips[k][c : c + 1, :]) for c in block]
        left = [[spread(rows[c][:, first + m : first + m + 1]) for m in range(c + 1)] for c in block]
        rows = [jnp.where(inside, jnp.where(lane == first + c, 1.0, 0.0), rows[c]) for c in block]
        lower = [[None] * SUBLANES for _ in block]
        solved = [None] * SUBLANES
        scaled = [None] * SUBLANES
        for p in range(0, SUBLANES, 2):
            later = range(p + 2, SUBLANES)
            a, b, c = left[p][p], left[p + 1][p], left[p + 1][p + 1]
            inverse = 1.0 / (a * c - b * b)
            one = {i: left[i][p] * c - left[i][p + 1] * b for i in later}
            two = {i: left[i][p + 1] * a - left[i][p] * b for i in later}
            for i in later:
                for m in range(p + 2, i + 1):
                    left[i][m] = left[i][m] - (one[i] * left[m][p] + two[i] * left[m][p + 1]) * inverse
                lower[i][p], lower[i][p + 1] = one[i] * inverse, two[i] * inverse
                rows[i] = rows[i] - (lower[i][p] * rows[p] + lower[i][p + 1] * rows[p + 1])
            solved[p] = (c * rows[p] - b * rows[p + 1]) * inverse
            solved[p + 1] = (a * rows[p + 1] - b * rows[p]) * inverse
            ratio = b / a
            scaled[p] = rows[p] * lax.rsqrt(a)
            scaled[p + 1] = (rows[p + 1] - ratio * rows[p]) * lax.rsqrt(c - b * ratio)
        for c in reversed(range(SUBLANES - 2)):
            solved[c] = solved[c] - tree_sum(lower[i][c] * solved[i] for i in range(c // 2 * 2 + 2, SUBLANES))
        for n in range(k + 1, LANES // SUBLANES):
            taken = tree_sum(spread(strips[n][:, first + c : first + c + 1]) * solved[c] for c in block)
            strips[n] = jnp.where(inside, 0.0, strips[n]) - taken
        result = scaled[0]
        for c in range(1, SUBLANES):
            result = jnp.where(row == c, scaled[c], result)
        done.append(jnp.where(lane <= row + first, result, 0.0) * across)
    return done


def inverse_factor_kernel(sums_ref, inverse_ref):
    top = sums_ref.shape[0] - LANES
    strips = [sums_ref[top + r : top + r + SUBLANES, :] for r in range(0, LANES, SUBLANES)]
    for r, strip in enumerate(inverse_factor(strips)):
        inverse_ref[r * SUBLANES : (r + 1) * SUBLANES, :] = strip


def invert_gram(sums):
    return pl.pallas_call(
        inverse_factor_kernel,
        in_specs=[WHOLE],
        out_specs=WHOLE,
        out_shape=near_shape((LANES, LANES)),
        cost_estimate=pl.CostEstimate(flops=6_000_000_000, bytes_accessed=200_000, transcendentals=20_000),
    )(near(sums))


def right_kernel(sums_ref, other_ref, inverse_ref, right_ref, squares_ref):
    half = other_ref.shape[0]
    core = lax.axis_index("core")
    inverse = inverse_ref[...]
    mine = product(sums_ref[:half, :], inverse, ROWS_BY_ROWS, HIGH)
    other = product(other_ref[...], inverse, ROWS_BY_ROWS, HIGH)
    right_ref[pl.ds(pl.multiple_of(core * half, half), half), :] = mine
    right_ref[pl.ds(pl.multiple_of((1 - core) * half, half), half), :] = other
    squares = jnp.sum(mine * mine, axis=0, keepdims=True) + jnp.sum(other * other, axis=0, keepdims=True)
    squares_ref[...] = jnp.broadcast_to(squares, squares_ref.shape)


def scale_right(sums, other, inverse, n_cols):
    height, width = 2 * other.shape[0], other.shape[1]
    return pl.pallas_call(
        right_kernel,
        in_specs=[WHOLE] * 3,
        out_specs=[WHOLE] * 2,
        out_shape=[near_shape((height, width)), jax.ShapeDtypeStruct((n_cols, width), jnp.float32)],
        cost_estimate=estimate(2 * height * width * width, 16 * height * width),
    )(near(sums), near(other), near(inverse))


def momentum_kernel(projected_ref, inverse_ref, right_ref, blend_ref, ortho_ref, next_ref, result, sems):
    ortho = product(projected_ref[...], inverse_ref[...], ROWS_BY_ROWS, HIGH)
    ortho_ref[...] = ortho
    right_high, right_low = high_low(right_ref[...])
    right_deep = jnp.concatenate([right_high, right_high], axis=1)
    step = ortho.shape[0] // sems.shape[0]
    copies = []
    for n in range(sems.shape[0]):
        rows = slice(n * step, (n + 1) * step)
        high, low = high_low(ortho[rows])
        outer = product(jnp.concatenate([high, low], axis=1), right_deep, ROWS_BY_ROWS) + product(high, right_low, ROWS_BY_ROWS)
        result[rows, :] = blend_ref[rows, :] - 0.05 * outer
        copies.append(pltpu.make_async_copy(result.at[rows], next_ref.at[rows], sems.at[n]))
        copies[-1].start()
    for copy in copies:
        copy.wait()


def step_momentum(projected, inverse, right, blend):
    return pl.pallas_call(
        momentum_kernel,
        in_specs=[WHOLE] * 4,
        out_specs=[WHOLE, FAR],
        out_shape=[near_shape(projected.shape), jax.ShapeDtypeStruct(blend.shape, jnp.float32)],
        scratch_shapes=[pltpu.VMEM(blend.shape, jnp.float32), pltpu.SemaphoreType.DMA((2,))],
        compiler_params=pltpu.CompilerParams(vmem_limit_bytes=VMEM_LIMIT),
        cost_estimate=estimate(2 * blend.size * projected.shape[1], 8 * blend.size),
    )(near(projected), near(inverse), near(right), near(blend))


def weight_kernel(total_rows, total_cols, ortho_ref, right_ref, squares_ref, weight_ref, basis_next_ref, next_ref, basis, result, sems):
    colsq = jnp.sum(squares_ref[...], axis=0, keepdims=True)
    scaled = right_ref[...] * lax.rsqrt(colsq * (1.0 / total_cols) + 1e-06)
    basis[...] = scaled
    copies = [pltpu.make_async_copy(basis, basis_next_ref, sems.at[0])]
    copies[0].start()
    scaled_high, scaled_low = high_low(scaled)
    scaled_deep = jnp.concatenate([scaled_high, scaled_high], axis=1)
    factor = 0.05 * (total_rows / scaled.shape[1]) ** 0.5
    parts = sems.shape[0] - 1
    step = ortho_ref.shape[0] // parts
    for n in range(parts):
        rows = slice(n * step, (n + 1) * step)
        high, low = high_low(ortho_ref[rows, :])
        outer = product(jnp.concatenate([high, low], axis=1), scaled_deep, ROWS_BY_ROWS) + product(high, scaled_low, ROWS_BY_ROWS)
        result[rows, :] = (weight_ref[rows, :].astype(jnp.float32) - factor * outer).astype(jnp.bfloat16)
        copies.append(pltpu.make_async_copy(result.at[rows], next_ref.at[rows], sems.at[n + 1]))
        copies[-1].start()
    for copy in copies:
        copy.wait()


def step_weight(total_rows, total_cols, ortho, right, squares, weight):
    return pl.pallas_call(
        functools.partial(weight_kernel, total_rows, total_cols),
        in_specs=[WHOLE] * 4,
        out_specs=[FAR] * 2,
        out_shape=[jax.ShapeDtypeStruct(right.shape, jnp.float32), jax.ShapeDtypeStruct(weight.shape, weight.dtype)],
        scratch_shapes=[
            pltpu.VMEM(right.shape, jnp.float32),
            pltpu.VMEM(weight.shape, weight.dtype),
            pltpu.SemaphoreType.DMA((3,)),
        ],
        compiler_params=pltpu.CompilerParams(vmem_limit_bytes=VMEM_LIMIT),
        cost_estimate=estimate(2 * weight.size * right.shape[1], 4 * weight.size),
    )(near(ortho), near(right), near(squares), near(weight))


def shards(momentum, gradient, basis, weight):
    rows, cols = momentum.shape
    rank = basis.shape[1]
    n_cols = lax.axis_size(COLS_AXES)
    total_rows = rows * lax.axis_size(ROWS_AXES)
    total_cols = cols * n_cols

    blend, partial_rows = project(momentum, gradient, basis)
    projected = all_sum(partial_rows.reshape(n_cols, rows // n_cols, rank), COLS_AXES).reshape(rows, rank)
    sums, other = sum_over_rows(blend, projected)
    inverse = invert_gram(sums)
    right, squares = scale_right(sums, other, inverse, n_cols)
    squares = lax.all_to_all(squares.reshape(n_cols, 1, rank), COLS_AXES, 0, 0).reshape(n_cols, rank)
    ortho, momentum_next = step_momentum(projected, inverse, right, blend)
    basis_next, weight_next = step_weight(total_rows, total_cols, ortho, right, squares, weight)
    return (momentum_next, basis_next, weight_next)


def split(mesh, x_size):
    n_rows, n_cols = mesh.devices.shape
    return Mesh(mesh.devices.reshape(n_rows // 2, 2, n_cols // x_size, x_size), ROWS_AXES + COLS_AXES)


def solution(mesh, x_size=4):
    block = P(ROWS_AXES, COLS_AXES)
    factor_block = P(COLS_AXES, None)
    return jax.shard_map(
        shards,
        mesh=split(mesh, x_size),
        in_specs=(block, block, factor_block, block),
        out_specs=(block, factor_block, block),
        check_vma=False,
    )
```

```python
import functools

import jax
import jax.numpy as jnp
from jax import lax
from jax.experimental import pallas as pl
from jax.experimental.pallas import tpu as pltpu
from jax.sharding import Mesh, PartitionSpec as P

ROWS_AXES = ("z", "core")
COLS_AXES = ("y", "x")
HIGH = lax.Precision.HIGHEST
SUBLANES = 8
VMEM_LIMIT = 32 * 1024 * 1024
LANES = 128
SWAP = [(0, 1), (1, 0)]


WHOLE = pl.BlockSpec(memory_space=pltpu.VMEM)
FAR = pl.BlockSpec(memory_space=pltpu.HBM)
ROWS_BY_COLS = ((1,), (0,))
ROWS_BY_ROWS = ((1,), (1,))
COLS_BY_COLS = ((0,), (0,))


def near_shape(shape):
    return pltpu.VMEM(shape, jnp.float32)


def near(array):
    return pltpu.with_memory_space_constraint(array, pltpu.VMEM)


def far(array):
    return pltpu.with_memory_space_constraint(array, pltpu.HBM)


def estimate(flops, bytes_accessed):
    return pl.CostEstimate(flops=flops, bytes_accessed=bytes_accessed, transcendentals=0)


def product(left, right, dims, precision=None):
    return lax.dot_general(left, right, (dims, ((), ())), precision=precision, preferred_element_type=jnp.float32)


def high_low(array):
    high = array.astype(jnp.bfloat16)
    return high, (array - high.astype(jnp.float32)).astype(jnp.bfloat16)


def pair(array):
    return jnp.concatenate(high_low(array), axis=1)


def split_product(left, right_pair, dims):
    high, low = high_low(left)
    total = product(high, right_pair, dims) + product(low, right_pair, dims)
    width = total.shape[1] // 2
    return total[:, :width] + total[:, width:]


def project_kernel(momentum_ref, gradient_ref, basis_ref, blend_ref, partial_ref, momentum, gradient, basis, sems):
    copies = [
        pltpu.make_async_copy(basis_ref, basis, sems.at[0]),
        pltpu.make_async_copy(momentum_ref, momentum, sems.at[1]),
        pltpu.make_async_copy(gradient_ref, gradient, sems.at[2]),
    ]
    for copy in copies:
        copy.start()
    copies[0].wait()
    basis_pair = pair(basis[...])
    copies[1].wait()
    copies[2].wait()
    blend = momentum[...] + gradient[...].astype(jnp.float32)
    blend_ref[...] = blend
    partial_ref[...] = split_product(blend, basis_pair, ROWS_BY_COLS)


def project(momentum, gradient, basis):
    return pl.pallas_call(
        project_kernel,
        in_specs=[FAR] * 3,
        out_specs=[WHOLE] * 2,
        out_shape=[near_shape(momentum.shape), near_shape((momentum.shape[0], basis.shape[1]))],
        scratch_shapes=[
            pltpu.VMEM(momentum.shape, momentum.dtype),
            pltpu.VMEM(gradient.shape, gradient.dtype),
            pltpu.VMEM(basis.shape, basis.dtype),
            pltpu.SemaphoreType.DMA((3,)),
        ],
        compiler_params=pltpu.CompilerParams(vmem_limit_bytes=VMEM_LIMIT),
        cost_estimate=estimate(2 * momentum.size * basis.shape[1], 8 * momentum.size),
    )(far(momentum), far(gradient), far(basis))


def half_of(ref, core):
    half = ref.shape[1] // 2
    return ref[:, pl.ds(pl.multiple_of(core * half, half), half)]


def sent_kernel(blend_ref, projected_ref, sent_ref):
    projected = projected_ref[...]
    half = blend_ref.shape[1] // 2
    blend = half_of(blend_ref, 1 - lax.axis_index("core"))
    sent_ref[:half, :] = split_product(blend, pair(projected), COLS_BY_COLS)
    sent_ref[half:, :] = product(projected, projected, COLS_BY_COLS, HIGH)


def kept_kernel(blend_ref, projected_ref, kept_ref):
    blend = half_of(blend_ref, lax.axis_index("core"))
    kept_ref[...] = split_product(blend, pair(projected_ref[...]), COLS_BY_COLS)


def right_terms(kernel, height, blend, projected):
    return pl.pallas_call(
        kernel,
        in_specs=[WHOLE] * 2,
        out_specs=WHOLE,
        out_shape=near_shape((height, projected.shape[1])),
        compiler_params=pltpu.CompilerParams(vmem_limit_bytes=VMEM_LIMIT),
        cost_estimate=estimate(blend.size * projected.shape[1], 4 * blend.size),
    )(near(blend), near(projected))


def sum_and_copy_kernel(parts_ref, copies_ref):
    total = parts_ref[0]
    for d in range(1, parts_ref.shape[0]):
        total = total + parts_ref[d]
    for d in range(copies_ref.shape[0]):
        copies_ref[d] = total


def all_sum(parts, axes):
    parts = lax.all_to_all(parts, axes, 0, 0)
    copies = pl.pallas_call(
        sum_and_copy_kernel,
        in_specs=[WHOLE],
        out_specs=WHOLE,
        out_shape=near_shape(parts.shape),
        cost_estimate=pl.CostEstimate(flops=parts.size, bytes_accessed=8 * parts.size, transcendentals=0),
    )(near(parts))
    return lax.all_to_all(copies, axes, 0, 0)


def sum_over_rows(blend, projected):
    half, width = blend.shape[1] // 2, projected.shape[1]
    sent = right_terms(sent_kernel, half + width, blend, projected)
    arrived = lax.ppermute(sent, "core", SWAP)
    kept = right_terms(kept_kernel, half, blend, projected)
    sums = jnp.concatenate([kept, sent[half:]]) + arrived
    ring = lax.axis_size("z")
    used = sums.shape[0]
    share = -(-used // (ring * SUBLANES)) * SUBLANES
    sums = jnp.pad(sums, ((0, ring * share - used), (0, 0)))
    sums = all_sum(sums.reshape(ring, share, width), "z").reshape(ring * share, width)[:used]
    return sums, lax.ppermute(sums[:half], "core", SWAP)


def spread(value):
    return jnp.broadcast_to(value, (SUBLANES, value.shape[-1] if value.shape[-1] > 1 else LANES))


def tree_sum(terms):
    terms = list(terms)
    while len(terms) > 1:
        terms = [sum(terms[i : i + 2][1:], terms[i]) for i in range(0, len(terms), 2)]
    return terms[0]


def inverse_factor(strips):
    lane = lax.broadcasted_iota(jnp.int32, (SUBLANES, LANES), 1)
    row = lax.broadcasted_iota(jnp.int32, (SUBLANES, LANES), 0)
    block = range(SUBLANES)
    diagonals = [jnp.where(lane == row + k * SUBLANES, strip, 0.0) for k, strip in enumerate(strips)]
    across = lax.rsqrt(spread(jnp.sum(tree_sum(diagonals), axis=0, keepdims=True)))
    strips = [
        strip * lax.rsqrt(spread(jnp.sum(diagonal, axis=1, keepdims=True))) * across
        for strip, diagonal in zip(strips, diagonals)
    ]
    done = []
    for k in range(LANES // SUBLANES):
        first = k * SUBLANES
        inside = (lane >= first) & (lane < first + SUBLANES)
        rows = [spread(strips[k][c : c + 1, :]) for c in block]
        left = [[spread(rows[c][:, first + m : first + m + 1]) for m in range(c + 1)] for c in block]
        rows = [jnp.where(inside, jnp.where(lane == first + c, 1.0, 0.0), rows[c]) for c in block]
        lower = [[None] * SUBLANES for _ in block]
        solved = [None] * SUBLANES
        scaled = [None] * SUBLANES
        for p in range(0, SUBLANES, 2):
            later = range(p + 2, SUBLANES)
            a, b, c = left[p][p], left[p + 1][p], left[p + 1][p + 1]
            inverse = 1.0 / (a * c - b * b)
            one = {i: left[i][p] * c - left[i][p + 1] * b for i in later}
            two = {i: left[i][p + 1] * a - left[i][p] * b for i in later}
            for i in later:
                for m in range(p + 2, i + 1):
                    left[i][m] = left[i][m] - (one[i] * left[m][p] + two[i] * left[m][p + 1]) * inverse
                lower[i][p], lower[i][p + 1] = one[i] * inverse, two[i] * inverse
                rows[i] = rows[i] - (lower[i][p] * rows[p] + lower[i][p + 1] * rows[p + 1])
            solved[p] = (c * rows[p] - b * rows[p + 1]) * inverse
            solved[p + 1] = (a * rows[p + 1] - b * rows[p]) * inverse
            ratio = b / a
            scaled[p] = rows[p] * lax.rsqrt(a)
            scaled[p + 1] = (rows[p + 1] - ratio * rows[p]) * lax.rsqrt(c - b * ratio)
        unit = {}
        for i in range(2, SUBLANES):
            for c in range(i // 2 * 2):
                between = range(c // 2 * 2 + 2, i // 2 * 2)
                unit[i, c] = -sum((lower[i][j] * unit[j, c] for j in between), lower[i][c])
        for c in range(SUBLANES - 2):
            terms = [unit[i, c] * solved[i] for i in range(c // 2 * 2 + 2, SUBLANES)]
            early = tree_sum([solved[c]] + terms[:-2])
            solved[c] = early + (terms[-2] + terms[-1])
        for n in range(k + 1, LANES // SUBLANES):
            taken = tree_sum(spread(strips[n][:, first + c : first + c + 1]) * solved[c] for c in block)
            strips[n] = jnp.where(inside, 0.0, strips[n]) - taken
        result = scaled[0]
        for c in range(1, SUBLANES):
            result = jnp.where(row == c, scaled[c], result)
        done.append(jnp.where(lane <= row + first, result, 0.0) * across)
    return done


def inverse_factor_kernel(sums_ref, inverse_ref):
    top = sums_ref.shape[0] - LANES
    strips = [sums_ref[top + r : top + r + SUBLANES, :] for r in range(0, LANES, SUBLANES)]
    for r, strip in enumerate(inverse_factor(strips)):
        inverse_ref[r * SUBLANES : (r + 1) * SUBLANES, :] = strip


def invert_gram(sums):
    return pl.pallas_call(
        inverse_factor_kernel,
        in_specs=[WHOLE],
        out_specs=WHOLE,
        out_shape=near_shape((LANES, LANES)),
        cost_estimate=pl.CostEstimate(flops=6_000_000_000, bytes_accessed=200_000, transcendentals=20_000),
    )(near(sums))


def right_kernel(sums_ref, other_ref, inverse_ref, right_ref, squares_ref):
    half = other_ref.shape[0]
    core = lax.axis_index("core")
    inverse = inverse_ref[...]
    mine = product(sums_ref[:half, :], inverse, ROWS_BY_ROWS, HIGH)
    other = product(other_ref[...], inverse, ROWS_BY_ROWS, HIGH)
    right_ref[pl.ds(pl.multiple_of(core * half, half), half), :] = mine
    right_ref[pl.ds(pl.multiple_of((1 - core) * half, half), half), :] = other
    squares = jnp.sum(mine * mine, axis=0, keepdims=True) + jnp.sum(other * other, axis=0, keepdims=True)
    squares_ref[...] = jnp.broadcast_to(squares, squares_ref.shape)


def scale_right(sums, other, inverse, n_cols):
    height, width = 2 * other.shape[0], other.shape[1]
    return pl.pallas_call(
        right_kernel,
        in_specs=[WHOLE] * 3,
        out_specs=[WHOLE] * 2,
        out_shape=[near_shape((height, width)), jax.ShapeDtypeStruct((n_cols, width), jnp.float32)],
        cost_estimate=estimate(2 * height * width * width, 16 * height * width),
    )(near(sums), near(other), near(inverse))


def momentum_kernel(projected_ref, inverse_ref, right_ref, blend_ref, ortho_ref, next_ref, result, sems):
    ortho = product(projected_ref[...], inverse_ref[...], ROWS_BY_ROWS, HIGH)
    ortho_ref[...] = ortho
    right_high, right_low = high_low(right_ref[...])
    right_deep = jnp.concatenate([right_high, right_high], axis=1)
    step = ortho.shape[0] // sems.shape[0]
    copies = []
    for n in range(sems.shape[0]):
        rows = slice(n * step, (n + 1) * step)
        high, low = high_low(ortho[rows])
        outer = product(jnp.concatenate([high, low], axis=1), right_deep, ROWS_BY_ROWS) + product(high, right_low, ROWS_BY_ROWS)
        result[rows, :] = blend_ref[rows, :] - 0.05 * outer
        copies.append(pltpu.make_async_copy(result.at[rows], next_ref.at[rows], sems.at[n]))
        copies[-1].start()
    for copy in copies:
        copy.wait()


def step_momentum(projected, inverse, right, blend):
    return pl.pallas_call(
        momentum_kernel,
        in_specs=[WHOLE] * 4,
        out_specs=[WHOLE, FAR],
        out_shape=[near_shape(projected.shape), jax.ShapeDtypeStruct(blend.shape, jnp.float32)],
        scratch_shapes=[pltpu.VMEM(blend.shape, jnp.float32), pltpu.SemaphoreType.DMA((2,))],
        compiler_params=pltpu.CompilerParams(vmem_limit_bytes=VMEM_LIMIT),
        cost_estimate=estimate(2 * blend.size * projected.shape[1], 8 * blend.size),
    )(near(projected), near(inverse), near(right), near(blend))


def weight_kernel(total_rows, total_cols, ortho_ref, right_ref, squares_ref, weight_ref, basis_next_ref, next_ref, basis, result, sems):
    colsq = jnp.sum(squares_ref[...], axis=0, keepdims=True)
    scaled = right_ref[...] * lax.rsqrt(colsq * (1.0 / total_cols) + 1e-06)
    basis[...] = scaled
    copies = [pltpu.make_async_copy(basis, basis_next_ref, sems.at[0])]
    copies[0].start()
    scaled_high, scaled_low = high_low(scaled)
    scaled_deep = jnp.concatenate([scaled_high, scaled_high], axis=1)
    factor = 0.05 * (total_rows / scaled.shape[1]) ** 0.5
    parts = sems.shape[0] - 1
    step = ortho_ref.shape[0] // parts
    for n in range(parts):
        rows = slice(n * step, (n + 1) * step)
        high, low = high_low(ortho_ref[rows, :])
        outer = product(jnp.concatenate([high, low], axis=1), scaled_deep, ROWS_BY_ROWS) + product(high, scaled_low, ROWS_BY_ROWS)
        result[rows, :] = (weight_ref[rows, :].astype(jnp.float32) - factor * outer).astype(jnp.bfloat16)
        copies.append(pltpu.make_async_copy(result.at[rows], next_ref.at[rows], sems.at[n + 1]))
        copies[-1].start()
    for copy in copies:
        copy.wait()


def step_weight(total_rows, total_cols, ortho, right, squares, weight):
    return pl.pallas_call(
        functools.partial(weight_kernel, total_rows, total_cols),
        in_specs=[WHOLE] * 4,
        out_specs=[FAR] * 2,
        out_shape=[jax.ShapeDtypeStruct(right.shape, jnp.float32), jax.ShapeDtypeStruct(weight.shape, weight.dtype)],
        scratch_shapes=[
            pltpu.VMEM(right.shape, jnp.float32),
            pltpu.VMEM(weight.shape, weight.dtype),
            pltpu.SemaphoreType.DMA((3,)),
        ],
        compiler_params=pltpu.CompilerParams(vmem_limit_bytes=VMEM_LIMIT),
        cost_estimate=estimate(2 * weight.size * right.shape[1], 4 * weight.size),
    )(near(ortho), near(right), near(squares), near(weight))


def shards(momentum, gradient, basis, weight):
    rows, cols = momentum.shape
    rank = basis.shape[1]
    n_cols = lax.axis_size(COLS_AXES)
    total_rows = rows * lax.axis_size(ROWS_AXES)
    total_cols = cols * n_cols

    blend, partial_rows = project(momentum, gradient, basis)
    projected = all_sum(partial_rows.reshape(n_cols, rows // n_cols, rank), COLS_AXES).reshape(rows, rank)
    sums, other = sum_over_rows(blend, projected)
    inverse = invert_gram(sums)
    right, squares = scale_right(sums, other, inverse, n_cols)
    squares = lax.all_to_all(squares.reshape(n_cols, 1, rank), COLS_AXES, 0, 0).reshape(n_cols, rank)
    ortho, momentum_next = step_momentum(projected, inverse, right, blend)
    basis_next, weight_next = step_weight(total_rows, total_cols, ortho, right, squares, weight)
    return (momentum_next, basis_next, weight_next)


def split(mesh, x_size):
    n_rows, n_cols = mesh.devices.shape
    return Mesh(mesh.devices.reshape(n_rows // 2, 2, n_cols // x_size, x_size), ROWS_AXES + COLS_AXES)


def solution(mesh, x_size=4):
    block = P(ROWS_AXES, COLS_AXES)
    factor_block = P(COLS_AXES, None)
    return jax.shard_map(
        shards,
        mesh=split(mesh, x_size),
        in_specs=(block, block, factor_block, block),
        out_specs=(block, factor_block, block),
        check_vma=False,
    )
```

```python
import functools

import jax
import jax.numpy as jnp
from jax import lax
from jax.experimental import pallas as pl
from jax.experimental.pallas import tpu as pltpu
from jax.sharding import Mesh, PartitionSpec as P

ROWS_AXES = ("z", "core")
COLS_AXES = ("y", "x")
HIGH = lax.Precision.HIGHEST
SUBLANES = 8
VMEM_LIMIT = 32 * 1024 * 1024
LANES = 128
SWAP = [(0, 1), (1, 0)]


WHOLE = pl.BlockSpec(memory_space=pltpu.VMEM)
FAR = pl.BlockSpec(memory_space=pltpu.HBM)
ROWS_BY_COLS = ((1,), (0,))
ROWS_BY_ROWS = ((1,), (1,))
COLS_BY_COLS = ((0,), (0,))


def near_shape(shape):
    return pltpu.VMEM(shape, jnp.float32)


def near(array):
    return pltpu.with_memory_space_constraint(array, pltpu.VMEM)


def far(array):
    return pltpu.with_memory_space_constraint(array, pltpu.HBM)


def estimate(flops, bytes_accessed):
    return pl.CostEstimate(flops=flops, bytes_accessed=bytes_accessed, transcendentals=0)


def product(left, right, dims, precision=None):
    return lax.dot_general(left, right, (dims, ((), ())), precision=precision, preferred_element_type=jnp.float32)


def high_low(array):
    high = array.astype(jnp.bfloat16)
    return high, (array - high.astype(jnp.float32)).astype(jnp.bfloat16)


def pair(array):
    return jnp.concatenate(high_low(array), axis=1)


def split_product(left, right_pair, dims):
    high, low = high_low(left)
    total = product(high, right_pair, dims) + product(low, right_pair, dims)
    width = total.shape[1] // 2
    return total[:, :width] + total[:, width:]


def project_kernel(momentum_ref, gradient_ref, basis_ref, blend_ref, partial_ref, momentum, gradient, basis, sems):
    parts = sems.shape[0] - 2
    step = momentum.shape[0] // parts
    rows = [slice(n * step, (n + 1) * step) for n in range(parts)]
    copies = [pltpu.make_async_copy(basis_ref, basis, sems.at[0]), pltpu.make_async_copy(gradient_ref, gradient, sems.at[1])]
    copies += [pltpu.make_async_copy(momentum_ref.at[r], momentum.at[r], sems.at[n + 2]) for n, r in enumerate(rows)]
    for copy in copies:
        copy.start()
    copies[0].wait()
    copies[1].wait()
    basis_pair = pair(basis[...])
    blends = []
    for r, copy in zip(rows, copies[2:]):
        copy.wait()
        blend = momentum[r, :] + gradient[r, :].astype(jnp.float32)
        blend_ref[r, :] = blend
        blends.append(pair(blend))
    total = product(jnp.concatenate(blends), jnp.concatenate([basis_pair, basis_pair]), ROWS_BY_COLS)
    width = basis.shape[1]
    partial_ref[...] = total[:, :width] + total[:, width:]


def project(momentum, gradient, basis):
    return pl.pallas_call(
        project_kernel,
        in_specs=[FAR] * 3,
        out_specs=[WHOLE] * 2,
        out_shape=[near_shape(momentum.shape), near_shape((momentum.shape[0], basis.shape[1]))],
        scratch_shapes=[
            pltpu.VMEM(momentum.shape, momentum.dtype),
            pltpu.VMEM(gradient.shape, gradient.dtype),
            pltpu.VMEM(basis.shape, basis.dtype),
            pltpu.SemaphoreType.DMA((4,)),
        ],
        compiler_params=pltpu.CompilerParams(vmem_limit_bytes=VMEM_LIMIT),
        cost_estimate=estimate(2 * momentum.size * basis.shape[1], 8 * momentum.size),
    )(far(momentum), far(gradient), far(basis))


def half_of(ref, core):
    half = ref.shape[1] // 2
    return ref[:, pl.ds(pl.multiple_of(core * half, half), half)]


def sent_kernel(blend_ref, projected_ref, sent_ref):
    projected = projected_ref[...]
    half = blend_ref.shape[1] // 2
    blend = half_of(blend_ref, 1 - lax.axis_index("core"))
    sent_ref[:half, :] = split_product(blend, pair(projected), COLS_BY_COLS)
    sent_ref[half:, :] = product(projected, projected, COLS_BY_COLS, HIGH)


def kept_kernel(blend_ref, projected_ref, kept_ref):
    blend = half_of(blend_ref, lax.axis_index("core"))
    kept_ref[...] = split_product(blend, pair(projected_ref[...]), COLS_BY_COLS)


def right_terms(kernel, height, blend, projected):
    return pl.pallas_call(
        kernel,
        in_specs=[WHOLE] * 2,
        out_specs=WHOLE,
        out_shape=near_shape((height, projected.shape[1])),
        compiler_params=pltpu.CompilerParams(vmem_limit_bytes=VMEM_LIMIT),
        cost_estimate=estimate(blend.size * projected.shape[1], 4 * blend.size),
    )(near(blend), near(projected))


def sum_and_copy_kernel(parts_ref, copies_ref):
    total = parts_ref[0]
    for d in range(1, parts_ref.shape[0]):
        total = total + parts_ref[d]
    for d in range(copies_ref.shape[0]):
        copies_ref[d] = total


def all_sum(parts, axes):
    parts = lax.all_to_all(parts, axes, 0, 0)
    copies = pl.pallas_call(
        sum_and_copy_kernel,
        in_specs=[WHOLE],
        out_specs=WHOLE,
        out_shape=near_shape(parts.shape),
        cost_estimate=pl.CostEstimate(flops=parts.size, bytes_accessed=8 * parts.size, transcendentals=0),
    )(near(parts))
    return lax.all_to_all(copies, axes, 0, 0)


def sum_over_rows(blend, projected):
    half, width = blend.shape[1] // 2, projected.shape[1]
    sent = right_terms(sent_kernel, half + width, blend, projected)
    arrived = lax.ppermute(sent, "core", SWAP)
    kept = right_terms(kept_kernel, half, blend, projected)
    sums = jnp.concatenate([kept, sent[half:]]) + arrived
    ring = lax.axis_size("z")
    used = sums.shape[0]
    share = -(-used // (ring * SUBLANES)) * SUBLANES
    sums = jnp.pad(sums, ((0, ring * share - used), (0, 0)))
    sums = all_sum(sums.reshape(ring, share, width), "z").reshape(ring * share, width)[:used]
    return sums, lax.ppermute(sums[:half], "core", SWAP)


def spread(value):
    return jnp.broadcast_to(value, (SUBLANES, value.shape[-1] if value.shape[-1] > 1 else LANES))


def tree_sum(terms):
    terms = list(terms)
    while len(terms) > 1:
        terms = [sum(terms[i : i + 2][1:], terms[i]) for i in range(0, len(terms), 2)]
    return terms[0]


def inverse_factor(strips):
    lane = lax.broadcasted_iota(jnp.int32, (SUBLANES, LANES), 1)
    row = lax.broadcasted_iota(jnp.int32, (SUBLANES, LANES), 0)
    block = range(SUBLANES)
    diagonals = [jnp.where(lane == row + k * SUBLANES, strip, 0.0) for k, strip in enumerate(strips)]
    across = lax.rsqrt(spread(jnp.sum(tree_sum(diagonals), axis=0, keepdims=True)))
    strips = [
        strip * lax.rsqrt(spread(jnp.sum(diagonal, axis=1, keepdims=True))) * across
        for strip, diagonal in zip(strips, diagonals)
    ]
    done = []
    for k in range(LANES // SUBLANES):
        first = k * SUBLANES
        inside = (lane >= first) & (lane < first + SUBLANES)
        rows = [spread(strips[k][c : c + 1, :]) for c in block]
        left = [[spread(rows[c][:, first + m : first + m + 1]) for m in range(c + 1)] for c in block]
        rows = [jnp.where(inside, jnp.where(lane == first + c, 1.0, 0.0), rows[c]) for c in block]
        lower = [[None] * SUBLANES for _ in block]
        solved = [None] * SUBLANES
        scaled = [None] * SUBLANES
        for p in range(0, SUBLANES, 2):
            later = range(p + 2, SUBLANES)
            a, b, c = left[p][p], left[p + 1][p], left[p + 1][p + 1]
            inverse = 1.0 / (a * c - b * b)
            one = {i: left[i][p] * c - left[i][p + 1] * b for i in later}
            two = {i: left[i][p + 1] * a - left[i][p] * b for i in later}
            for i in later:
                for m in range(p + 2, i + 1):
                    left[i][m] = left[i][m] - (one[i] * left[m][p] + two[i] * left[m][p + 1]) * inverse
                lower[i][p], lower[i][p + 1] = one[i] * inverse, two[i] * inverse
                rows[i] = rows[i] - (lower[i][p] * rows[p] + lower[i][p + 1] * rows[p + 1])
            solved[p] = (c * rows[p] - b * rows[p + 1]) * inverse
            solved[p + 1] = (a * rows[p + 1] - b * rows[p]) * inverse
            ratio = b / a
            scaled[p] = rows[p] * lax.rsqrt(a)
            scaled[p + 1] = (rows[p + 1] - ratio * rows[p]) * lax.rsqrt(c - b * ratio)
        unit = {}
        for i in range(2, SUBLANES):
            for c in range(i // 2 * 2):
                between = range(c // 2 * 2 + 2, i // 2 * 2)
                unit[i, c] = -sum((lower[i][j] * unit[j, c] for j in between), lower[i][c])
        for c in range(SUBLANES - 2):
            terms = [unit[i, c] * solved[i] for i in range(c // 2 * 2 + 2, SUBLANES)]
            early = tree_sum([solved[c]] + terms[:-2])
            solved[c] = early + (terms[-2] + terms[-1])
        for n in range(k + 1, LANES // SUBLANES):
            taken = tree_sum(spread(strips[n][:, first + c : first + c + 1]) * solved[c] for c in block)
            strips[n] = jnp.where(inside, 0.0, strips[n]) - taken
        result = scaled[0]
        for c in range(1, SUBLANES):
            result = jnp.where(row == c, scaled[c], result)
        done.append(jnp.where(lane <= row + first, result, 0.0) * across)
    return done


def inverse_factor_kernel(sums_ref, inverse_ref):
    top = sums_ref.shape[0] - LANES
    strips = [sums_ref[top + r : top + r + SUBLANES, :] for r in range(0, LANES, SUBLANES)]
    for r, strip in enumerate(inverse_factor(strips)):
        inverse_ref[r * SUBLANES : (r + 1) * SUBLANES, :] = strip


def invert_gram(sums):
    return pl.pallas_call(
        inverse_factor_kernel,
        in_specs=[WHOLE],
        out_specs=WHOLE,
        out_shape=near_shape((LANES, LANES)),
        cost_estimate=pl.CostEstimate(flops=6_000_000_000, bytes_accessed=200_000, transcendentals=20_000),
    )(near(sums))


def right_kernel(sums_ref, other_ref, inverse_ref, right_ref, squares_ref):
    half = other_ref.shape[0]
    core = lax.axis_index("core")
    inverse = inverse_ref[...]
    mine = product(sums_ref[:half, :], inverse, ROWS_BY_ROWS, HIGH)
    other = product(other_ref[...], inverse, ROWS_BY_ROWS, HIGH)
    right_ref[pl.ds(pl.multiple_of(core * half, half), half), :] = mine
    right_ref[pl.ds(pl.multiple_of((1 - core) * half, half), half), :] = other
    squares = jnp.sum(mine * mine, axis=0, keepdims=True) + jnp.sum(other * other, axis=0, keepdims=True)
    squares_ref[...] = jnp.broadcast_to(squares, squares_ref.shape)


def scale_right(sums, other, inverse, n_cols):
    height, width = 2 * other.shape[0], other.shape[1]
    return pl.pallas_call(
        right_kernel,
        in_specs=[WHOLE] * 3,
        out_specs=[WHOLE] * 2,
        out_shape=[near_shape((height, width)), jax.ShapeDtypeStruct((n_cols, width), jnp.float32)],
        cost_estimate=estimate(2 * height * width * width, 16 * height * width),
    )(near(sums), near(other), near(inverse))


def momentum_kernel(projected_ref, inverse_ref, right_ref, blend_ref, ortho_ref, next_ref, result, sems):
    ortho = product(projected_ref[...], inverse_ref[...], ROWS_BY_ROWS, HIGH)
    ortho_ref[...] = ortho
    right_high, right_low = high_low(right_ref[...])
    right_deep = jnp.concatenate([right_high, right_high], axis=1)
    step = ortho.shape[0] // sems.shape[0]
    copies = []
    for n in range(sems.shape[0]):
        rows = slice(n * step, (n + 1) * step)
        high, low = high_low(ortho[rows])
        outer = product(jnp.concatenate([high, low], axis=1), right_deep, ROWS_BY_ROWS) + product(high, right_low, ROWS_BY_ROWS)
        result[rows, :] = blend_ref[rows, :] - 0.05 * outer
        copies.append(pltpu.make_async_copy(result.at[rows], next_ref.at[rows], sems.at[n]))
        copies[-1].start()
    for copy in copies:
        copy.wait()


def step_momentum(projected, inverse, right, blend):
    return pl.pallas_call(
        momentum_kernel,
        in_specs=[WHOLE] * 4,
        out_specs=[WHOLE, FAR],
        out_shape=[near_shape(projected.shape), jax.ShapeDtypeStruct(blend.shape, jnp.float32)],
        scratch_shapes=[pltpu.VMEM(blend.shape, jnp.float32), pltpu.SemaphoreType.DMA((2,))],
        compiler_params=pltpu.CompilerParams(vmem_limit_bytes=VMEM_LIMIT),
        cost_estimate=estimate(2 * blend.size * projected.shape[1], 8 * blend.size),
    )(near(projected), near(inverse), near(right), near(blend))


def weight_kernel(total_rows, total_cols, ortho_ref, right_ref, squares_ref, weight_ref, basis_next_ref, next_ref, basis, result, sems):
    colsq = jnp.sum(squares_ref[...], axis=0, keepdims=True)
    scaled = right_ref[...] * lax.rsqrt(colsq * (1.0 / total_cols) + 1e-06)
    basis[...] = scaled
    copies = [pltpu.make_async_copy(basis, basis_next_ref, sems.at[0])]
    copies[0].start()
    scaled_high, scaled_low = high_low(scaled)
    scaled_deep = jnp.concatenate([scaled_high, scaled_high], axis=1)
    factor = 0.05 * (total_rows / scaled.shape[1]) ** 0.5
    parts = sems.shape[0] - 1
    step = ortho_ref.shape[0] // parts
    for n in range(parts):
        rows = slice(n * step, (n + 1) * step)
        high, low = high_low(ortho_ref[rows, :])
        outer = product(jnp.concatenate([high, low], axis=1), scaled_deep, ROWS_BY_ROWS) + product(high, scaled_low, ROWS_BY_ROWS)
        result[rows, :] = (weight_ref[rows, :].astype(jnp.float32) - factor * outer).astype(jnp.bfloat16)
        copies.append(pltpu.make_async_copy(result.at[rows], next_ref.at[rows], sems.at[n + 1]))
        copies[-1].start()
    for copy in copies:
        copy.wait()


def step_weight(total_rows, total_cols, ortho, right, squares, weight):
    return pl.pallas_call(
        functools.partial(weight_kernel, total_rows, total_cols),
        in_specs=[WHOLE] * 4,
        out_specs=[FAR] * 2,
        out_shape=[jax.ShapeDtypeStruct(right.shape, jnp.float32), jax.ShapeDtypeStruct(weight.shape, weight.dtype)],
        scratch_shapes=[
            pltpu.VMEM(right.shape, jnp.float32),
            pltpu.VMEM(weight.shape, weight.dtype),
            pltpu.SemaphoreType.DMA((3,)),
        ],
        compiler_params=pltpu.CompilerParams(vmem_limit_bytes=VMEM_LIMIT),
        cost_estimate=estimate(2 * weight.size * right.shape[1], 4 * weight.size),
    )(near(ortho), near(right), near(squares), near(weight))


def shards(momentum, gradient, basis, weight):
    rows, cols = momentum.shape
    rank = basis.shape[1]
    n_cols = lax.axis_size(COLS_AXES)
    total_rows = rows * lax.axis_size(ROWS_AXES)
    total_cols = cols * n_cols

    blend, partial_rows = project(momentum, gradient, basis)
    projected = all_sum(partial_rows.reshape(n_cols, rows // n_cols, rank), COLS_AXES).reshape(rows, rank)
    sums, other = sum_over_rows(blend, projected)
    inverse = invert_gram(sums)
    right, squares = scale_right(sums, other, inverse, n_cols)
    squares = lax.all_to_all(squares.reshape(n_cols, 1, rank), COLS_AXES, 0, 0).reshape(n_cols, rank)
    ortho, momentum_next = step_momentum(projected, inverse, right, blend)
    basis_next, weight_next = step_weight(total_rows, total_cols, ortho, right, squares, weight)
    return (momentum_next, basis_next, weight_next)


def split(mesh, x_size):
    n_rows, n_cols = mesh.devices.shape
    return Mesh(mesh.devices.reshape(n_rows // 2, 2, n_cols // x_size, x_size), ROWS_AXES + COLS_AXES)


def solution(mesh, x_size=4):
    block = P(ROWS_AXES, COLS_AXES)
    factor_block = P(COLS_AXES, None)
    return jax.shard_map(
        shards,
        mesh=split(mesh, x_size),
        in_specs=(block, block, factor_block, block),
        out_specs=(block, factor_block, block),
        check_vma=False,
    )
```
